128 devices in a mesh: row: 8 (over z, y_hi), col: 8 (over x, y_lo), dp: 2 (over core).
Axes of the slice: x: 4, y: 4 (y_hi: 2, y_lo: 2; y = y_hi * 2 + y_lo), z: 4, core: 2. Of those that a mesh axis runs over, the one named last changes fastest.
Arguments:
- tokens: bfloat16 [2048, 6144], P(('dp', 'col'), 'row'), may hold values from -6 to 6
- up_weight: bfloat16 [6144, 24576], P('row', 'col'), may hold values from -0.078125 to 0.078125
- down_weight: bfloat16 [24576, 6144], P('col', 'row'), may hold values from -0.0390625 to 0.0390625
- cotangent: bfloat16 [2048, 6144], P(('dp', 'col'), 'row'), may hold values from -6 to 6
Outputs:
- mlp_output: bfloat16 [2048, 6144], P(('dp', 'col'), 'row')
- input_grad: bfloat16 [2048, 6144], P(('dp', 'col'), 'row')
- up_grad: float32 [6144, 24576], P('row', ('col', 'dp'))
- down_grad: float32 [24576, 6144], P(('col', 'dp'), 'row')
The draws below stay inside these ranges and needn't reach their ends.
All inputs are finite; a program needn't handle non-finite values.
Results may differ from the reference program's by a relative error of at most 0.03.
Values may be sent and summed in bfloat16 or wider, within the bound.
A program may use at most 192 MiB of HBM per device.

```python
import jax
import jax.numpy as jnp
from jax import lax

D = 6144
FF = 24576
TOKENS = 2048
N_ROW = 8
N_COL = 8


def levels(stream_key, extent, cuts, smallest, high):
    gain = 1.0
    for axis_at, shards_of in cuts:
        heights = jax.random.uniform(jax.random.fold_in(jax.random.fold_in(stream_key, 6), axis_at), (shards_of,), jnp.float32, smallest / len(cuts), high / len(cuts))
        gain = gain * jnp.repeat(jnp.exp(heights), extent[axis_at] // shards_of).reshape((-1,) + (1,) * (len(extent) - 1 - axis_at))
    return gain


def normal_values(own_key, extent, width, limit, split=(), kind=jnp.bfloat16):
    loudness = levels(own_key, extent, split, -0.22, 0.18) if split else 1.0
    array = jax.random.normal(own_key, extent, jnp.float32) * width * loudness
    return jnp.minimum(jnp.maximum(array, -limit), limit).astype(kind)


def setup_inputs(seed: int = 0) -> dict:
    streams_of = jax.random.split(jax.random.key(seed), 5)
    return {
        "tokens": normal_values(streams_of[0], (TOKENS, D), 1.0, 6.0, ((0, 16), (1, 8))),
        "up_weight": normal_values(streams_of[1], (D, FF), D ** -0.5, 0.078125, ((0, 8), (1, 8))),
        "down_weight": normal_values(streams_of[2], (FF, D), FF ** -0.5, 0.0390625, ((0, 8), (1, 8))),
        "cotangent": normal_values(streams_of[3], (TOKENS, D), 1.0, 6.0, ((0, 16), (1, 8))),
    }


ROOT_HALF = 0.7071067811865476
DENSITY = 0.3989422804014327


def gelu_exact(values):
    return 0.5 * values * (1.0 + lax.erf(values * ROOT_HALF))


def gelu_slope(values):
    return 0.5 * (1.0 + lax.erf(values * ROOT_HALF)) + values * DENSITY * jnp.exp(-0.5 * values * values)


def rounded(values):
    return lax.optimization_barrier(values.astype(jnp.bfloat16)).astype(jnp.float32)


def contract_last(matrix_a, matrix_b):
    return lax.dot_general(matrix_a, matrix_b, (((1,), (1,)), ((), ())), preferred_element_type=jnp.float32)


def contract_first(matrix_a, matrix_b):
    return lax.dot_general(matrix_a, matrix_b, (((0,), (0,)), ((), ())), preferred_element_type=jnp.float32)


def reference(tokens, up_weight, down_weight, cotangent):
    feat_block = D // N_ROW
    hidden_block = FF // N_COL
    preact = jnp.zeros((TOKENS, FF), jnp.float32)
    slope_in = jnp.zeros((TOKENS, FF), jnp.float32)
    for number in range(N_ROW):
        offset = number * feat_block
        preact = preact + rounded(jnp.dot(tokens[:, offset:offset + feat_block], up_weight[offset:offset + feat_block], preferred_element_type=jnp.float32))
        slope_in = slope_in + rounded(contract_last(cotangent[:, offset:offset + feat_block], down_weight[:, offset:offset + feat_block]))
    activated = gelu_exact(preact).astype(jnp.bfloat16)
    hidden_grad = (slope_in * gelu_slope(preact)).astype(jnp.bfloat16)
    mixed_out = jnp.zeros((TOKENS, D), jnp.float32)
    input_sum = jnp.zeros((TOKENS, D), jnp.float32)
    for number in range(N_COL):
        offset = number * hidden_block
        mixed_out = mixed_out + rounded(jnp.dot(activated[:, offset:offset + hidden_block], down_weight[offset:offset + hidden_block], preferred_element_type=jnp.float32))
        input_sum = input_sum + rounded(contract_last(hidden_grad[:, offset:offset + hidden_block], up_weight[:, offset:offset + hidden_block]))
    up_grad = contract_first(tokens, hidden_grad)
    down_grad = contract_first(activated, cotangent)
    return mixed_out.astype(jnp.bfloat16), input_sum.astype(jnp.bfloat16), up_grad, down_grad
```

```python
import jax
import jax.numpy as jnp
from jax import lax
from jax.sharding import Mesh, PartitionSpec as P

ROOT_HALF = 0.7071067811865476
DENSITY = 0.3989422804014327


def contract_last(matrix_a, matrix_b):
    return lax.dot_general(
        matrix_a, matrix_b, (((1,), (1,)), ((), ())), preferred_element_type=jnp.float32
    )


def contract_first(matrix_a, matrix_b):
    return lax.dot_general(
        matrix_a, matrix_b, (((0,), (0,)), ((), ())), preferred_element_type=jnp.float32
    )


def on_device(tokens, up_weight, down_weight, cotangent):
    yh = lax.axis_index("yh")
    half = up_weight.shape[1] // 2
    gathered, incoming = (
        lax.all_gather(lax.all_gather(part, "yh", axis=1, tiled=True), ("x", "yl"), axis=0, tiled=True)
        for part in (tokens, cotangent)
    )
    swap = [(0, 1), (1, 0)]
    up_mine = lax.dynamic_slice_in_dim(up_weight, yh * half, half, 1)
    up_theirs = lax.ppermute(lax.dynamic_slice_in_dim(up_weight, (1 - yh) * half, half, 1), "yh", swap)
    down_mine = lax.dynamic_slice_in_dim(down_weight, yh * half, half, 0)
    down_theirs = lax.ppermute(
        lax.dynamic_slice_in_dim(down_weight, (1 - yh) * half, half, 0), "yh", swap
    )
    up = jnp.where(
        yh == 0,
        jnp.concatenate([up_mine, up_theirs], 0),
        jnp.concatenate([up_theirs, up_mine], 0),
    )
    down = jnp.where(
        yh == 0,
        jnp.concatenate([down_mine, down_theirs], 1),
        jnp.concatenate([down_theirs, down_mine], 1),
    )
    bf = jnp.bfloat16
    partial_up = jnp.dot(gathered, up, preferred_element_type=jnp.float32).astype(bf)
    partial_back = contract_last(incoming, down).astype(bf)
    preact = lax.psum_scatter(partial_up, "z", scatter_dimension=0, tiled=True).astype(jnp.float32)
    back_sum = lax.psum_scatter(partial_back, "z", scatter_dimension=0, tiled=True).astype(jnp.float32)
    cdf = 0.5 * (1.0 + lax.erf(preact * ROOT_HALF))
    activated = (preact * cdf).astype(bf)
    hidden_grad = (back_sum * (cdf + preact * DENSITY * jnp.exp(-0.5 * preact * preact))).astype(bf)
    activated = lax.all_gather(activated, "z", axis=0, tiled=True)
    hidden_grad = lax.all_gather(hidden_grad, "z", axis=0, tiled=True)

    def spread(part):
        part = lax.psum_scatter(part.astype(bf), "yh", scatter_dimension=1, tiled=True)
        return lax.psum_scatter(part, ("x", "yl"), scatter_dimension=0, tiled=True)

    mlp_output = spread(jnp.dot(activated, down, preferred_element_type=jnp.float32))
    input_grad = spread(contract_last(hidden_grad, up))
    across = [(0, 0), (1, 2), (2, 1), (3, 3)]
    up_grad = lax.psum_scatter(
        contract_first(gathered, hidden_grad).astype(bf), "dp", scatter_dimension=0, tiled=True
    )
    up_grad = lax.ppermute(up_grad, ("yh", "dp"), across)
    down_grad = lax.psum_scatter(
        contract_first(activated, incoming).astype(bf), "dp", scatter_dimension=1, tiled=True
    )
    down_grad = lax.ppermute(down_grad, ("yh", "dp"), across)
    return (mlp_output, input_grad, up_grad.astype(jnp.float32), down_grad.astype(jnp.float32))


def solution(mesh):
    fine = Mesh(mesh.devices.reshape(4, 2, 4, 2, 2), ("z", "yh", "x", "yl", "dp"))
    rows = P(("dp", "x", "yl"), ("z", "yh"))
    return jax.shard_map(
        on_device,
        mesh=fine,
        in_specs=(rows, P(("z", "yh"), ("x", "yl")), P(("x", "yl"), ("z", "yh")), rows),
        out_specs=(rows, rows, P(("z", "yh"), ("x", "yl", "dp")), P(("x", "yl", "dp"), ("z", "yh"))),
        check_vma=False,
    )
```

```python
import functools

import jax
import jax.numpy as jnp
from jax import lax
from jax.experimental import pallas as pl
from jax.experimental.pallas import tpu as pltpu
from jax.sharding import Mesh, PartitionSpec as P

ROOT_HALF = 0.7071067811865476
DENSITY = 0.3989422804014327
AXES = ("z", "yh", "x", "yl", "dp")
BF, F32 = jnp.bfloat16, jnp.float32

NP = 2
TB = 64
TP = 8 * TB
DB = 768
HB = 1536
CH = 256
NCH = HB // CH
NIT = NP * NCH
SLOTS = 6
ZB = TP // 4
TH = TB // 2
AG_STEPS = 5
RS_STEPS = 5
LAG = 4


def nt(a, b):
    return lax.dot_general(a, b, (((1,), (1,)), ((), ())), preferred_element_type=F32)


def tn(a, b):
    return lax.dot_general(a, b, (((0,), (0,)), ((), ())), preferred_element_type=F32)


def nn(a, b):
    return jnp.dot(a, b, preferred_element_type=F32)


def kernel(
    tok, cot, w1, w2, mlp, ig, ug, dg,
    xg, gg, w1c, w2c, ph, r1, r2, ab, yacc, dacc, py, e1, e2, f1, f2,
    st1, st2, rt1, rt2, ow1, ow2,
    own_sem, wl_sem, ws_sem, wr_sem, as_sem, ar_sem,
    zs_sem, zr_sem, gs_sem, gr_sem, ps_sem, pr_sem, ds_sem, dr_sem, os_sem, or_sem,
):
    z, yh, x, yl, k = (lax.axis_index(a) for a in AXES)
    y = yh * 2 + yl

    def up(v, n):
        return lax.rem(v + n, 4)

    z1, z2, z3 = up(z, 1), up(z, 2), up(z, 3)
    x1, x2, x3 = up(x, 1), up(x, 2), up(x, 3)
    y1, y3 = up(y, 1), up(y, 3)
    yh1, yl1, yh3, yl3 = y1 // 2, lax.rem(y1, 2), y3 // 2, lax.rem(y3, 2)
    yo, ko = 1 - yh, 1 - k
    z_dev = ((z1, yh, x, yl, k), (z3, yh, x, yl, k))
    x_dev = ((z, yh, x1, yl, k), (z, yh, x3, yl, k))
    y_dev = ((z, yh1, x, yl1, k), (z, yh3, x, yl3, k))
    far = (z, yo, x, yl, k)
    sib = (z, yh, x, yl, ko)
    diag = (z, yo, x, yl, ko)

    def send(src, dst, s_sem, r_sem, device):
        return pltpu.make_async_remote_copy(
            src_ref=src, dst_ref=dst, send_sem=s_sem, recv_sem=r_sem,
            device_id=device, device_id_type=pl.DeviceIdType.MESH,
        )

    def own(p):
        rows = pl.ds(p * TB, TB)
        return (
            pltpu.make_async_copy(tok.at[rows], xg.at[yh, p, x, yl], own_sem.at[p, 0]),
            pltpu.make_async_copy(cot.at[rows], gg.at[yh, p, x, yl], own_sem.at[p, 1]),
        )

    def hidden_at(half, c):
        return pl.multiple_of(half * HB + c * CH, CH)

    def w_own(c):
        return (
            pltpu.make_async_copy(w1.at[:, pl.ds(hidden_at(yh, c), CH)], w1c.at[c, yh], wl_sem.at[c, 0]),
            pltpu.make_async_copy(w2.at[pl.ds(hidden_at(yh, c), CH)], w2c.at[c, yh], wl_sem.at[c, 1]),
        )

    r_half = pl.ds(pl.multiple_of(k * (DB // 2), DB // 2), DB // 2)
    h_half = pl.ds(pl.multiple_of(k * (CH // 2), CH // 2), CH // 2)

    def w_far(c):
        rows = pl.ds(pl.multiple_of(yo * HB + c * CH + k * (CH // 2), CH // 2), CH // 2)
        return (
            send(w1.at[r_half, pl.ds(hidden_at(yo, c), CH)], w1c.at[c, yh, r_half],
                 ws_sem.at[c, 0, 0], wr_sem.at[c, 0, 0], far),
            send(w2.at[rows], w2c.at[c, yh, h_half], ws_sem.at[c, 0, 1], wr_sem.at[c, 0, 1], far),
        )

    def w_sib(c):
        return tuple(
            send(ref.at[c, yo, part], ref.at[c, yo, part], ws_sem.at[c, 1, a], wr_sem.at[c, 1, a], sib)
            for a, (ref, part) in enumerate(((w1c, r_half), (w2c, h_half)))
        )

    def ag(p, s):
        if s == 0:
            pairs = [[xg.at[yh, p, x, yl]] * 2, [gg.at[yh, p, x, yl]] * 2]
        elif s == 1:
            pairs = [
                [xg.at[yh, p, x3, yl, pl.ds(0, TH)], xg.at[yh, p, x1, yl, pl.ds(TH, TH)]],
                [gg.at[yh3, p, x, yl3, pl.ds(0, TH)], gg.at[yh1, p, x, yl1, pl.ds(TH, TH)]],
            ]
        elif s == 2:
            pairs = [[xg.at[yh, p, :, yl]] * 2, [gg.at[:, p, x]] * 2]
        else:
            pairs = [
                [xg.at[yh3, p, pl.ds(0, 2), yl3], xg.at[yh1, p, pl.ds(2, 2), yl1]],
                [gg.at[0, p, x3], gg.at[1, p, x1]],
            ]
        over = (x_dev, y_dev) if s < 2 else (y_dev, x_dev)
        return [
            send(pairs[a][d], pairs[a][d], as_sem.at[p, s, a, d], ar_sem.at[p, s, a, d], over[a][d])
            for a in range(2) for d in range(2)
        ]

    def ag_step(p, s):
        if s == 0:
            for copy in own(p):
                copy.wait()
        else:
            for copy in ag(p, s - 1):
                copy.wait_recv()
        if s < 4:
            for copy in ag(p, s):
                copy.start()

    def rs1(j):
        slot = lax.rem(j, SLOTS)
        return [
            send(ph.at[slot, :, z2, pl.ds(d * (ZB // 2), ZB // 2)], r1.at[j, d],
                 zs_sem.at[slot, 0, d], zr_sem.at[j, 0, d], z_dev[d])
            for d in range(2)
        ]

    def rs2(j):
        slot = lax.rem(j, SLOTS)
        return [
            send(ph.at[slot, :, (z1, z3)[d]], r2.at[j, d], zs_sem.at[slot, 1, d], zr_sem.at[j, 1, d], z_dev[d])
            for d in range(2)
        ]

    def ag1(j):
        p, c = j // NCH, lax.rem(j, NCH)
        part = ab.at[c, :, p, z]
        return [send(part, part, gs_sem.at[j, 0, d], gr_sem.at[j, 0, d], z_dev[d]) for d in range(2)]

    def ag2(j):
        p, c = j // NCH, lax.rem(j, NCH)
        parts = (
            ab.at[c, :, p, z3, pl.ds(0, ZB // 2)],
            ab.at[c, :, p, z1, pl.ds(ZB // 2, ZB // 2)],
        )
        return [
            send(parts[d], parts[d], gs_sem.at[j, 1, d], gr_sem.at[j, 1, d], z_dev[d]) for d in range(2)
        ]

    def start_item(j):
        p, c = j // NCH, lax.rem(j, NCH)
        slot = lax.rem(j, SLOTS)

        @pl.when(p == 0)
        def _():
            for copy in w_own(c):
                copy.wait()
            for copy in w_sib(c):
                copy.wait_recv()

        @pl.when(j >= SLOTS)
        def _():
            for copy in rs1(j - SLOTS) + rs2(j - SLOTS):
                copy.wait_send()

        h = nn(xg[0, p].reshape(TP, DB), w1c[c, 0])
        h = h + nn(xg[1, p].reshape(TP, DB), w1c[c, 1])
        ph[slot, 0] = h.astype(BF).reshape(4, ZB, CH)
        s = nt(gg[0, p].reshape(TP, DB), w2c[c, 0])
        s = s + nt(gg[1, p].reshape(TP, DB), w2c[c, 1])
        ph[slot, 1] = s.astype(BF).reshape(4, ZB, CH)
        for copy in rs1(j):
            copy.start()

    def merge_item(j):
        slot = lax.rem(j, SLOTS)
        for d, (copy, go) in enumerate(zip(rs1(j), rs2(j))):
            copy.wait_recv()
            rows = pl.ds(d * (ZB // 2), ZB // 2)
            to = (z1, z3)[d]
            ph[slot, :, to, rows] = (
                ph[slot, :, to, rows].astype(F32) + r1[j, d].astype(F32)
            ).astype(BF)
            go.start()

    def gelu_item(j):
        p, c = j // NCH, lax.rem(j, NCH)
        slot = lax.rem(j, SLOTS)
        for copy in rs2(j):
            copy.wait_recv()
        pre = ph[slot, 0, z].astype(F32) + r2[j, 0, 0].astype(F32) + r2[j, 1, 0].astype(F32)
        back = ph[slot, 1, z].astype(F32) + r2[j, 0, 1].astype(F32) + r2[j, 1, 1].astype(F32)
        cdf = 0.5 * (1.0 + lax.erf(pre * ROOT_HALF))
        ab[c, 0, p, z] = (pre * cdf).astype(BF)
        ab[c, 1, p, z] = (back * (cdf + pre * DENSITY * jnp.exp(-0.5 * pre * pre))).astype(BF)
        for copy in ag1(j):
            copy.start()

    def spread_item(j):
        for copy, go in zip(ag1(j), ag2(j)):
            copy.wait_recv()
            go.start()

    def to_sib(c):
        slot = lax.rem(c, 2)
        return (
            send(st1.at[slot], rt1.at[c], ds_sem.at[slot, 0], dr_sem.at[c, 0], sib),
            send(st2.at[slot], rt2.at[c], ds_sem.at[slot, 1], dr_sem.at[c, 1], sib),
        )

    def out_parts(c):
        hid = pl.ds(pl.multiple_of(c * CH, CH), CH)
        return ((rt1.at[c], ug.at[:, hid]), (rt2.at[c], dg.at[hid]))

    def out_local(c):
        return [pltpu.make_async_copy(s, d, os_sem.at[c, a]) for a, (s, d) in enumerate(out_parts(c))]

    def out_far(c):
        return [send(s, d, os_sem.at[c, a], or_sem.at[c, a], diag) for a, (s, d) in enumerate(out_parts(c))]

    def use_item(j):
        p, c = j // NCH, lax.rem(j, NCH)
        for copy in ag2(j):
            copy.wait_recv()
        act = ab[c, 0, p].reshape(TP, CH)
        hid = ab[c, 1, p].reshape(TP, CH)

        @pl.when(c == 0)
        def _():
            for half in range(2):
                yacc[half] = nn(act, w2c[c, half])
                dacc[half] = nt(hid, w1c[c, half])

        @pl.when(c > 0)
        def _():
            for half in range(2):
                yacc[half] += nn(act, w2c[c, half])
                dacc[half] += nt(hid, w1c[c, half])

        @pl.when(p == NP - 1)
        def _():
            slot = lax.rem(c, 2)

            @pl.when(c >= 2)
            def _():
                for copy in to_sib(c - 2):
                    copy.wait_send()

            acts = ab[c, 0].reshape(NP * TP, CH)
            hids = ab[c, 1].reshape(NP * TP, CH)
            st1[slot] = tn(xg[ko].reshape(NP * TP, DB), hids).astype(BF)
            st2[slot] = tn(acts, gg[ko].reshape(NP * TP, DB)).astype(BF)
            for copy in to_sib(c):
                copy.start()
            ow1[...] = tn(xg[k].reshape(NP * TP, DB), hids)
            ow2[...] = tn(acts, gg[k].reshape(NP * TP, DB))

    def finish_grad(c):
        for copy in to_sib(c):
            copy.wait_recv()
        rt1[c] = (rt1[c].astype(F32) + ow1[...]).astype(BF)
        rt2[c] = (rt2[c].astype(F32) + ow2[...]).astype(BF)

        @pl.when(k == yh)
        def _():
            for copy in out_local(c):
                copy.start()

        @pl.when(k != yh)
        def _():
            for copy in out_far(c):
                copy.start()

    def rs(p, s):
        if s == 0:
            srcs = [
                [py.at[0, 0, x2], py.at[0, 1, x2]],
                [py.at[1, yo, pl.ds(0, 2), yl], py.at[1, yo, pl.ds(2, 2), yl]],
            ]
            dsts = e1
        elif s == 1:
            srcs = [
                [py.at[0, :, x1], py.at[0, :, x3]],
                [py.at[1, yh1, :, yl1], py.at[1, yh3, :, yl3]],
            ]
            dsts = None
        elif s == 2:
            srcs = [
                [py.at[0, yo, x, yl, pl.ds(0, TH)], py.at[0, yo, x, yl, pl.ds(TH, TH)]],
                [py.at[1, yh, x2, yl, pl.ds(0, TH)], py.at[1, yh, x2, yl, pl.ds(TH, TH)]],
            ]
            dsts = f1
        else:
            srcs = [
                [py.at[0, yh1, x, yl1], py.at[0, yh3, x, yl3]],
                [py.at[1, yh, x1, yl], py.at[1, yh, x3, yl]],
            ]
            dsts = f2
        over = (x_dev, y_dev) if s < 2 else (y_dev, x_dev)
        copies = []
        for a in range(2):
            for d in range(2):
                dst = dsts.at[p, a, d] if s != 1 else (e2a, e2b)[a].at[p, d]
                copies.append(send(srcs[a][d], dst, ps_sem.at[s, a, d], pr_sem.at[p, s, a, d], over[a][d]))
        return copies

    e2a, e2b = e2

    def bump(ref, index, more):
        ref[index] = (ref[index].astype(F32) + more.astype(F32)).astype(BF)

    def rs_step(p, s):
        if s == 0:
            for half in range(2):
                py[0, half] = yacc[half].astype(BF).reshape(4, 2, TB, DB)
                py[1, half] = dacc[half].astype(BF).reshape(4, 2, TB, DB)
        else:
            for copy in rs(p, s - 1):
                copy.wait_recv()
        if s == 1:
            bump(py, (0, 0, x1), e1[p, 0, 0])
            bump(py, (0, 1, x3), e1[p, 0, 1])
            bump(py, (1, yh1, pl.ds(0, 2), yl1), e1[p, 1, 0])
            bump(py, (1, yh3, pl.ds(2, 2), yl3), e1[p, 1, 1])
        elif s == 2:
            for half in range(2):
                py[0, half, x] = (
                    py[0, half, x].astype(F32) + e2a[p, 0, half].astype(F32) + e2a[p, 1, half].astype(F32)
                ).astype(BF)
            for at in range(4):
                py[1, yh, at, yl] = (
                    py[1, yh, at, yl].astype(F32) + e2b[p, 0, at].astype(F32) + e2b[p, 1, at].astype(F32)
                ).astype(BF)
        elif s == 3:
            low, high = pl.ds(0, TH), pl.ds(TH, TH)
            bump(py, (0, yh1, x, yl1, low), f1[p, 0, 0])
            bump(py, (0, yh3, x, yl3, high), f1[p, 0, 1])
            bump(py, (1, yh, x1, yl, low), f1[p, 1, 0])
            bump(py, (1, yh, x3, yl, high), f1[p, 1, 1])
        elif s == 4:
            rows = pl.ds(pl.multiple_of(p * TB, TB), TB)
            for a, out in enumerate((mlp, ig)):
                out[rows] = (
                    py[a, yh, x, yl].astype(F32) + f2[p, a, 0].astype(F32) + f2[p, a, 1].astype(F32)
                ).astype(BF)
            for at in range(4):
                for copy in rs(p, at):
                    copy.wait_send()
        if s < 4:
            for copy in rs(p, s):
                copy.start()

    barrier = pltpu.get_barrier_semaphore()
    peers = (*z_dev, *x_dev, *y_dev, far, sib, diag)
    for p in range(NP):
        for copy in own(p):
            copy.start()
    for c in range(NCH):
        for copy in w_own(c):
            copy.start()
    for device in peers:
        pl.semaphore_signal(barrier, inc=1, device_id=device, device_id_type=pl.DeviceIdType.MESH)
    pl.semaphore_wait(barrier, len(peers))

    for copy in w_far(0):
        copy.start()

    first = -AG_STEPS
    last = NIT + LAG - 1 + RS_STEPS

    def step(it, carry):
        i = it + first
        for s in range(AG_STEPS):
            @pl.when((lax.rem(it, AG_STEPS) == s) & (it < NP * AG_STEPS))
            def _():
                ag_step(it // AG_STEPS, s)

        @pl.when((i + 3 >= 1) & (i + 3 < NCH))
        def _():
            for copy in w_far(i + 3):
                copy.start()

        @pl.when((i + 1 >= 0) & (i + 1 < NCH))
        def _():
            for copy, go in zip(w_far(i + 1), w_sib(i + 1)):
                copy.wait_recv()
                go.start()

        @pl.when((i >= 1) & (i - 1 < NIT))
        def _():
            merge_item(i - 1)

        @pl.when((i >= 2) & (i - 2 < NIT))
        def _():
            gelu_item(i - 2)

        @pl.when((i >= 3) & (i - 3 < NIT))
        def _():
            spread_item(i - 3)

        @pl.when((i - LAG - 1 >= NIT - NCH) & (i - LAG - 1 < NIT))
        def _():
            finish_grad(i - LAG - 1 - (NIT - NCH))

        @pl.when((i >= 0) & (i < NIT))
        def _():
            start_item(i)

        @pl.when((i >= LAG) & (i - LAG < NIT))
        def _():
            use_item(i - LAG)

        q = i - (LAG + NCH - 1)
        for s in range(RS_STEPS):
            @pl.when((q >= 0) & (lax.rem(q + 2 * NCH, NCH) == s))
            def _():
                rs_step(q // NCH, s)

        return carry

    lax.fori_loop(0, last - first, step, 0)

    for p in range(NP):
        for s in range(4):
            for copy in ag(p, s):
                copy.wait_send()

    def drain(j, carry):
        for copy in ag1(j) + ag2(j):
            copy.wait_send()

        @pl.when(j >= NIT - SLOTS)
        def _():
            for copy in rs1(j) + rs2(j):
                copy.wait_send()

        @pl.when(j < NCH)
        def _():
            for copy in w_far(j) + w_sib(j):
                copy.wait_send()

            @pl.when(j >= NCH - 2)
            def _():
                for copy in to_sib(j):
                    copy.wait_send()

            @pl.when(k == yh)
            def _():
                for copy in out_local(j):
                    copy.wait()

            @pl.when(k != yh)
            def _():
                for copy in out_far(j):
                    copy.wait()

        return carry

    lax.fori_loop(0, NIT, drain, 0)


def on_device(tokens, up_weight, down_weight, cotangent):
    vmem, dma = pltpu.VMEM, pltpu.SemaphoreType.DMA
    anywhere = pl.BlockSpec(memory_space=pl.ANY)
    inside = pl.BlockSpec(memory_space=pltpu.VMEM)

    def body(*refs):
        refs = list(refs)
        at = 8 + 12
        kernel(*refs[:at], (refs[at], refs[at + 1]), *refs[at + 2:])

    mlp, ig, ug, dg = pl.pallas_call(
        body,
        out_shape=(
            jax.ShapeDtypeStruct((NP * TB, DB), BF),
            jax.ShapeDtypeStruct((NP * TB, DB), BF),
            jax.ShapeDtypeStruct((DB, HB), BF),
            jax.ShapeDtypeStruct((HB, DB), BF),
        ),
        in_specs=[anywhere] * 4,
        out_specs=(inside, inside, anywhere, anywhere),
        scratch_shapes=[
            vmem((2, NP, 4, 2, TB, DB), BF),
            vmem((2, NP, 4, 2, TB, DB), BF),
            vmem((NCH, 2, DB, CH), BF),
            vmem((NCH, 2, CH, DB), BF),
            vmem((SLOTS, 2, 4, ZB, CH), BF),
            vmem((NIT, 2, 2, ZB // 2, CH), BF),
            vmem((NIT, 2, 2, ZB, CH), BF),
            vmem((NCH, 2, NP, 4, ZB, CH), BF),
            vmem((2, TP, DB), F32),
            vmem((2, TP, DB), F32),
            vmem((2, 2, 4, 2, TB, DB), BF),
            vmem((NP, 2, 2, 2, TB, DB), BF),
            vmem((NP, 2, 2, 2, TB, DB), BF),
            vmem((NP, 2, 4, TB, DB), BF),
            vmem((NP, 2, 2, TH, DB), BF),
            vmem((NP, 2, 2, TB, DB), BF),
            vmem((2, DB, CH), BF),
            vmem((2, CH, DB), BF),
            vmem((NCH, DB, CH), BF),
            vmem((NCH, CH, DB), BF),
            vmem((DB, CH), F32),
            vmem((CH, DB), F32),
            dma((NP, 2)),
            dma((NCH, 2)),
            dma((NCH, 2, 2)),
            dma((NCH, 2, 2)),
            dma((NP, 4, 2, 2)),
            dma((NP, 4, 2, 2)),
            dma((SLOTS, 2, 2)),
            dma((NIT, 2, 2)),
            dma((NIT, 2, 2)),
            dma((NIT, 2, 2)),
            dma((4, 2, 2)),
            dma((NP, 4, 2, 2)),
            dma((2, 2)),
            dma((NCH, 2)),
            dma((NCH, 2)),
            dma((NCH, 2)),
        ],
        compiler_params=pltpu.CompilerParams(
            collective_id=0, has_side_effects=True, vmem_limit_bytes=62 * 2**20
        ),
        cost_estimate=pl.CostEstimate(flops=29 * 10**9, bytes_accessed=20 * 10**6, transcendentals=10**6),
        name="block",
    )(tokens, cotangent, up_weight, down_weight)
    return mlp, ig, ug.astype(F32), dg.astype(F32)


def solution(mesh):
    fine = Mesh(mesh.devices.reshape(4, 2, 4, 2, 2), AXES)
    rows = P(("dp", "x", "yl"), ("z", "yh"))
    return jax.shard_map(
        on_device,
        mesh=fine,
        in_specs=(rows, P(("z", "yh"), ("x", "yl")), P(("x", "yl"), ("z", "yh")), rows),
        out_specs=(rows, rows, P(("z", "yh"), ("x", "yl", "dp")), P(("x", "yl", "dp"), ("z", "yh"))),
        check_vma=False,
    )
```

```python
import functools

import jax
import jax.numpy as jnp
from jax import lax
from jax.experimental import pallas as pl
from jax.experimental.pallas import tpu as pltpu
from jax.sharding import Mesh, PartitionSpec as P

ROOT_HALF = 0.7071067811865476
DENSITY = 0.3989422804014327
AXES = ("z", "yh", "x", "yl", "dp")
BF, F32 = jnp.bfloat16, jnp.float32

NP = 4
AS = 2
TB = 32
TP = 8 * TB
DB = 768
HB = 1536
CH = 256
NCH = HB // CH
NIT = NP * NCH
ZB = TP // 4
TH = TB // 2
OPS = (
    "start", "merge", "gelu", "spread", "use", "w_far0", "w_far1", "w_sib0", "w_sib1", "w_wait",
    "ag0", "ag1", "ag2", "ag3", "ag_wait", "rs0", "rs1", "rs2", "rs3", "rs4", "dw", "fin", "nop",
)
STEPS = (
    320, 321, 160, 352, 353, 323, 192, 384, 355, 224, 322, 197, 385, 256, 165, 416,
    417, 354, 261, 288, 387, 161, 229, 386, 325, 448, 0, 193, 293, 5, 32, 419,
    324, 162, 37, 225, 418, 64, 257, 356, 69, 357, 194, 289, 449, 96, 11, 1,
    7, 164, 101, 6, 326, 43, 388, 33, 39, 38, 258, 327, 196, 226, 389, 75,
    65, 290, 8, 2, 228, 359, 70, 195, 71, 97, 421, 260, 34, 40, 420, 163,
    103, 102, 292, 10, 4, 66, 391, 259, 358, 128, 450, 107, 72, 227, 42, 134,
    98, 390, 36, 291, 3, 104, 9, 74, 423, 129, 35, 422, 68, 130, 41, 12,
    67, 133, 13, 100, 451, 19, 18, 99, 20, 44, 14, 132, 50, 131, 481, 106,
    73, 76, 480, 82, 51, 513, 135, 138, 105, 45, 139, 136, 108, 512, 114, 15,
    83, 137, 46, 77, 483, 140, 482, 146, 52, 640, 545, 115, 17, 544, 78, 109,
    21, 47, 84, 577, 147, 576, 672, 49, 515, 141, 641, 110, 16, 53, 116, 514,
    79, 81, 608, 142, 609, 547, 673, 48, 148, 85, 642, 111, 22, 546, 80, 117,
    23, 54, 113, 579, 674, 143, 112, 149, 55, 643, 86, 145, 144, 485, 87, 118,
    484, 578, 675, 119, 517, 150, 644, 611, 151, 516, 610, 487, 549, 676, 645, 486,
    519, 548, 677, 518, 551, 550, 580, 581, 583, 582, 613, 615, 612, 614,
)


def nt(a, b):
    return lax.dot_general(a, b, (((1,), (1,)), ((), ())), preferred_element_type=F32)


def tn(a, b):
    return lax.dot_general(a, b, (((0,), (0,)), ((), ())), preferred_element_type=F32)


def nn(a, b):
    return jnp.dot(a, b, preferred_element_type=F32)


def kernel(
    tok, cot, w1, w2, mlp, ig, ug, dg,
    tg, w1c, w2c, ph, r1, r2, ab, acc, py, e1, e2, f1, f2, st1, st2, rt1, rt2, ow1, ow2,
    own_sem, wl_sem, ws_sem, wr_sem, as_sem, ar_sem,
    zs_sem, zr_sem, gs_sem, gr_sem, ps_sem, pr_sem, ds_sem, dr_sem, os_sem, or_sem,
):
    z, yh, x, yl, k = (lax.axis_index(a) for a in AXES)
    y = yh * 2 + yl

    def up(v, n):
        return lax.rem(v + n, 4)

    z1, z2, z3 = up(z, 1), up(z, 2), up(z, 3)
    x1, x2, x3 = up(x, 1), up(x, 2), up(x, 3)
    y1, y3 = up(y, 1), up(y, 3)
    yh1, yl1, yh3, yl3 = y1 // 2, lax.rem(y1, 2), y3 // 2, lax.rem(y3, 2)
    yo, ko = 1 - yh, 1 - k
    z_dev = ((z1, yh, x, yl, k), (z3, yh, x, yl, k))
    x_dev = ((z, yh, x1, yl, k), (z, yh, x3, yl, k))
    y_dev = ((z, yh1, x, yl1, k), (z, yh3, x, yl3, k))
    far = (z, yo, x, yl, k)
    sib = (z, yh, x, yl, ko)
    diag = (z, yo, x, yl, ko)

    def send(src, dst, s_sem, r_sem, device):
        return pltpu.make_async_remote_copy(
            src_ref=src, dst_ref=dst, send_sem=s_sem, recv_sem=r_sem,
            device_id=device, device_id_type=pl.DeviceIdType.MESH,
        )

    def own(p, a):
        rows = pl.ds(pl.multiple_of(p * TB, TB), TB)
        return pltpu.make_async_copy((tok, cot)[a].at[rows], tg.at[a, yh, p, x, yl], own_sem.at[p, a])

    def hidden_at(half, c):
        return pl.multiple_of(half * HB + c * CH, CH)

    def w_own(c):
        return (
            pltpu.make_async_copy(w1.at[:, pl.ds(hidden_at(yh, c), CH)], w1c.at[c, yh], wl_sem.at[c, 0]),
            pltpu.make_async_copy(w2.at[pl.ds(hidden_at(yh, c), CH)], w2c.at[c, yh], wl_sem.at[c, 1]),
        )

    r_half = pl.ds(pl.multiple_of(k * (DB // 2), DB // 2), DB // 2)
    h_half = pl.ds(pl.multiple_of(k * (CH // 2), CH // 2), CH // 2)

    def w_far(c):
        rows = pl.ds(pl.multiple_of(yo * HB + c * CH + k * (CH // 2), CH // 2), CH // 2)
        return (
            send(w1.at[r_half, pl.ds(hidden_at(yo, c), CH)], w1c.at[c, yh, r_half],
                 ws_sem.at[c, 0, 0], wr_sem.at[c, 0, 0], far),
            send(w2.at[rows], w2c.at[c, yh, h_half], ws_sem.at[c, 0, 1], wr_sem.at[c, 0, 1], far),
        )

    def w_sib(c):
        return tuple(
            send(ref.at[c, yo, part], ref.at[c, yo, part], ws_sem.at[c, 1, a], wr_sem.at[c, 1, a], sib)
            for a, (ref, part) in enumerate(((w1c, r_half), (w2c, h_half)))
        )

    def ag(s, p, a):
        over = (y_dev, x_dev)[s // 2]
        if s == 0:
            parts = [tg.at[a, yh, p, x, yl]] * 2
        elif s == 1:
            parts = [tg.at[a, yh3, p, x, yl3, pl.ds(0, TH)], tg.at[a, yh1, p, x, yl1, pl.ds(TH, TH)]]
        elif s == 2:
            parts = [tg.at[a, :, p, x]] * 2
        else:
            parts = [tg.at[a, 0, p, x3], tg.at[a, 1, p, x1]]
        return [
            send(parts[d], parts[d], as_sem.at[p, s, a, d], ar_sem.at[p, s, a, d], over[d]) for d in range(2)
        ]

    def ag_step(s, arg):
        p, a = arg // 2, lax.rem(arg, 2)
        if s == 0:
            for b in range(2):
                @pl.when(a == b)
                def _():
                    own(p, b).wait()
        else:
            for copy in ag(s - 1, p, a):
                copy.wait_recv()
        for copy in ag(s, p, a):
            copy.start()

    def ag_wait(p):
        for a in range(2):
            for copy in ag(3, p, a):
                copy.wait_recv()

    def rs1(j):
        return [
            send(ph.at[j, :, z2, pl.ds(d * (ZB // 2), ZB // 2)], r1.at[j, d],
                 zs_sem.at[j, 0, d], zr_sem.at[j, 0, d], z_dev[d])
            for d in range(2)
        ]

    def rs2(j):
        return [
            send(ph.at[j, :, (z1, z3)[d]], r2.at[j, d], zs_sem.at[j, 1, d], zr_sem.at[j, 1, d], z_dev[d])
            for d in range(2)
        ]

    def ag1(j):
        p, c = j // NCH, lax.rem(j, NCH)
        part = ab.at[c, :, p, z]
        return [send(part, part, gs_sem.at[j, 0, d], gr_sem.at[j, 0, d], z_dev[d]) for d in range(2)]

    def ag2(j):
        p, c = j // NCH, lax.rem(j, NCH)
        parts = (
            ab.at[c, :, p, z3, pl.ds(0, ZB // 2)],
            ab.at[c, :, p, z1, pl.ds(ZB // 2, ZB // 2)],
        )
        return [
            send(parts[d], parts[d], gs_sem.at[j, 1, d], gr_sem.at[j, 1, d], z_dev[d]) for d in range(2)
        ]

    def start_item(j):
        p, c = j // NCH, lax.rem(j, NCH)
        h = nn(tg[0, 0, p].reshape(TP, DB), w1c[c, 0])
        h = h + nn(tg[0, 1, p].reshape(TP, DB), w1c[c, 1])
        ph[j, 0] = h.astype(BF).reshape(4, ZB, CH)
        s = nt(tg[1, 0, p].reshape(TP, DB), w2c[c, 0])
        s = s + nt(tg[1, 1, p].reshape(TP, DB), w2c[c, 1])
        ph[j, 1] = s.astype(BF).reshape(4, ZB, CH)
        for copy in rs1(j):
            copy.start()

    def merge_item(j):
        for d, (copy, go) in enumerate(zip(rs1(j), rs2(j))):
            copy.wait_recv()
            rows = pl.ds(d * (ZB // 2), ZB // 2)
            to = (z1, z3)[d]
            ph[j, :, to, rows] = (
                ph[j, :, to, rows].astype(F32) + r1[j, d].astype(F32)
            ).astype(BF)
            go.start()

    def gelu_item(j):
        p, c = j // NCH, lax.rem(j, NCH)
        for copy in rs2(j):
            copy.wait_recv()
        pre = ph[j, 0, z].astype(F32) + r2[j, 0, 0].astype(F32) + r2[j, 1, 0].astype(F32)
        back = ph[j, 1, z].astype(F32) + r2[j, 0, 1].astype(F32) + r2[j, 1, 1].astype(F32)
        cdf = 0.5 * (1.0 + lax.erf(pre * ROOT_HALF))
        ab[c, 0, p, z] = (pre * cdf).astype(BF)
        ab[c, 1, p, z] = (back * (cdf + pre * DENSITY * jnp.exp(-0.5 * pre * pre))).astype(BF)
        for copy in ag1(j):
            copy.start()

    def spread_item(j):
        for copy, go in zip(ag1(j), ag2(j)):
            copy.wait_recv()
            go.start()

    def to_sib(c):
        slot = lax.rem(c, 2)
        return (
            send(st1.at[slot], rt1.at[c], ds_sem.at[slot, 0], dr_sem.at[c, 0], sib),
            send(st2.at[slot], rt2.at[c], ds_sem.at[slot, 1], dr_sem.at[c, 1], sib),
        )

    def out_parts(c):
        hid = pl.ds(pl.multiple_of(c * CH, CH), CH)
        return ((rt1.at[c], ug.at[:, hid]), (rt2.at[c], dg.at[hid]))

    def out_local(c):
        return [pltpu.make_async_copy(s, d, os_sem.at[c, a]) for a, (s, d) in enumerate(out_parts(c))]

    def out_far(c):
        return [send(s, d, os_sem.at[c, a], or_sem.at[c, a], diag) for a, (s, d) in enumerate(out_parts(c))]

    def use_item(j):
        p, c = j // NCH, lax.rem(j, NCH)
        for copy in ag2(j):
            copy.wait_recv()
        act = ab[c, 0, p].reshape(TP, CH)
        hid = ab[c, 1, p].reshape(TP, CH)
        slot = lax.rem(p, AS)

        @pl.when(c == 0)
        def _():
            for half in range(2):
                acc[slot, 0, half] = nn(act, w2c[c, half])
                acc[slot, 1, half] = nt(hid, w1c[c, half])

        @pl.when(c > 0)
        def _():
            for half in range(2):
                acc[slot, 0, half] += nn(act, w2c[c, half])
                acc[slot, 1, half] += nt(hid, w1c[c, half])

    def grad_item(c):
        slot = lax.rem(c, 2)

        @pl.when(c >= 2)
        def _():
            for copy in to_sib(c - 2):
                copy.wait_send()

        acts = ab[c, 0].reshape(NP * TP, CH)
        hids = ab[c, 1].reshape(NP * TP, CH)
        st1[slot] = tn(tg[0, ko].reshape(NP * TP, DB), hids).astype(BF)
        st2[slot] = tn(acts, tg[1, ko].reshape(NP * TP, DB)).astype(BF)
        for copy in to_sib(c):
            copy.start()
        ow1[...] = tn(tg[0, k].reshape(NP * TP, DB), hids)
        ow2[...] = tn(acts, tg[1, k].reshape(NP * TP, DB))

    def finish_grad(c):
        for copy in to_sib(c):
            copy.wait_recv()
        rt1[c] = (rt1[c].astype(F32) + ow1[...]).astype(BF)
        rt2[c] = (rt2[c].astype(F32) + ow2[...]).astype(BF)

        @pl.when(k == yh)
        def _():
            for copy in out_local(c):
                copy.start()

        @pl.when(k != yh)
        def _():
            for copy in out_far(c):
                copy.start()

    def rs(s, p, a):
        over = (x_dev, y_dev)[s // 2]
        slot = lax.rem(p, AS)
        if s == 0:
            srcs = [py.at[slot, a, d, x2] for d in range(2)]
        elif s == 1:
            srcs = [py.at[slot, a, :, x1], py.at[slot, a, :, x3]]
        elif s == 2:
            srcs = [py.at[slot, a, yo, x, yl, pl.ds(d * TH, TH)] for d in range(2)]
        else:
            srcs = [py.at[slot, a, yh1, x, yl1], py.at[slot, a, yh3, x, yl3]]
        return [
            send(srcs[d], (e1, e2, f1, f2)[s].at[p, a, d], ps_sem.at[p, s, a, d], pr_sem.at[p, s, a, d], over[d])
            for d in range(2)
        ]

    def bump(ref, index, *more):
        total = ref[index].astype(F32)
        for term in more:
            total = total + term.astype(F32)
        ref[index] = total.astype(BF)

    def rs_step(s, arg):
        p, a = arg // 2, lax.rem(arg, 2)
        slot = lax.rem(p, AS)
        if s == 0:
            for half in range(2):
                py[slot, a, half] = acc[slot, a, half].astype(BF).reshape(4, 2, TB, DB)
        else:
            for copy in rs(s - 1, p, a):
                copy.wait_recv()
        if s == 1:
            bump(py, (slot, a, 0, x1), e1[p, a, 0])
            bump(py, (slot, a, 1, x3), e1[p, a, 1])
        elif s == 2:
            for half in range(2):
                bump(py, (slot, a, half, x), e2[p, a, 0, half], e2[p, a, 1, half])
        elif s == 3:
            bump(py, (slot, a, yh1, x, yl1, pl.ds(0, TH)), f1[p, a, 0])
            bump(py, (slot, a, yh3, x, yl3, pl.ds(TH, TH)), f1[p, a, 1])
        elif s == 4:
            rows = pl.ds(pl.multiple_of(p * TB, TB), TB)
            total = (
                py[slot, a, yh, x, yl].astype(F32) + f2[p, a, 0].astype(F32) + f2[p, a, 1].astype(F32)
            ).astype(BF)
            for b, out in enumerate((mlp, ig)):
                @pl.when(a == b)
                def _():
                    out[rows] = total
            for at in range(4):
                for copy in rs(at, p, a):
                    copy.wait_send()
        if s < 4:
            for copy in rs(s, p, a):
                copy.start()

    barrier = pltpu.get_barrier_semaphore()
    peers = (*z_dev, *x_dev, *y_dev, far, sib, diag)
    for p in range(NP):
        for a in range(2):
            own(p, a).start()
    for c in range(NCH):
        for copy in w_own(c):
            copy.start()
    for device in peers:
        pl.semaphore_signal(barrier, inc=1, device_id=device, device_id_type=pl.DeviceIdType.MESH)
    pl.semaphore_wait(barrier, len(peers))

    def w_far_step(a, c):
        w_far(c)[a].start()

    def w_sib_step(a, c):
        w_far(c)[a].wait_recv()
        w_sib(c)[a].start()

    def w_wait(c):
        for copy in w_own(c):
            copy.wait()
        for copy in w_sib(c):
            copy.wait_recv()

    runs = [start_item, merge_item, gelu_item, spread_item, use_item]
    runs += [functools.partial(w_far_step, a) for a in range(2)]
    runs += [functools.partial(w_sib_step, a) for a in range(2)]
    runs += [w_wait]
    runs += [functools.partial(ag_step, s) for s in range(4)]
    runs += [ag_wait]
    runs += [functools.partial(rs_step, s) for s in range(5)]
    runs += [grad_item, finish_grad]
    nop = OPS.index("nop")

    def dispatch(lo, hi, what, arg):
        if hi - lo == 1:
            if lo < nop:
                runs[lo](arg)
            return
        mid = (lo + hi) // 2

        @pl.when(what < mid)
        def _():
            dispatch(lo, mid, what, arg)

        @pl.when(what >= mid)
        def _():
            dispatch(mid, hi, what, arg)

    steps = list(STEPS) + [nop * 32] * (-len(STEPS) % 3)
    words = [steps[n] + steps[n + 1] * 1024 + steps[n + 2] * 1024 * 1024 for n in range(0, len(steps), 3)]

    def word(n, carry):
        value = jnp.int32(words[0])
        for at in range(1, len(words)):
            value = jnp.where(n == at, jnp.int32(words[at]), value)

        def step(_, left):
            now = lax.rem(left, 1024)
            dispatch(0, nop + 1, now // 32, lax.rem(now, 32))
            return left // 1024

        lax.fori_loop(0, 3, step, value)
        return carry

    lax.fori_loop(0, len(words), word, 0)

    def drain(j, carry):
        for copy in rs1(j) + rs2(j) + ag1(j) + ag2(j):
            copy.wait_send()

        @pl.when(j < NP * 2)
        def _():
            for s in range(4):
                for copy in ag(s, j // 2, lax.rem(j, 2)):
                    copy.wait_send()

        @pl.when(j < NCH)
        def _():
            for copy in w_far(j) + w_sib(j):
                copy.wait_send()

            @pl.when(j >= NCH - 2)
            def _():
                for copy in to_sib(j):
                    copy.wait_send()

            @pl.when(k == yh)
            def _():
                for copy in out_local(j):
                    copy.wait()

            @pl.when(k != yh)
            def _():
                for copy in out_far(j):
                    copy.wait()

        return carry

    lax.fori_loop(0, NIT, drain, 0)


def on_device(tokens, up_weight, down_weight, cotangent):
    vmem, dma = pltpu.VMEM, pltpu.SemaphoreType.DMA
    anywhere = pl.BlockSpec(memory_space=pl.ANY)
    inside = pl.BlockSpec(memory_space=pltpu.VMEM)

    mlp, ig, ug, dg = pl.pallas_call(
        kernel,
        out_shape=(
            jax.ShapeDtypeStruct((NP * TB, DB), BF),
            jax.ShapeDtypeStruct((NP * TB, DB), BF),
            jax.ShapeDtypeStruct((DB, HB), BF),
            jax.ShapeDtypeStruct((HB, DB), BF),
        ),
        in_specs=[anywhere] * 4,
        out_specs=(inside, inside, anywhere, anywhere),
        scratch_shapes=[
            vmem((2, 2, NP, 4, 2, TB, DB), BF),
            vmem((NCH, 2, DB, CH), BF),
            vmem((NCH, 2, CH, DB), BF),
            vmem((NIT, 2, 4, ZB, CH), BF),
            vmem((NIT, 2, 2, ZB // 2, CH), BF),
            vmem((NIT, 2, 2, ZB, CH), BF),
            vmem((NCH, 2, NP, 4, ZB, CH), BF),
            vmem((AS, 2, 2, TP, DB), F32),
            vmem((AS, 2, 2, 4, 2, TB, DB), BF),
            vmem((NP, 2, 2, 2, TB, DB), BF),
            vmem((NP, 2, 2, 2, 2, TB, DB), BF),
            vmem((NP, 2, 2, TH, DB), BF),
            vmem((NP, 2, 2, TB, DB), BF),
            vmem((2, DB, CH), BF),
            vmem((2, CH, DB), BF),
            vmem((NCH, DB, CH), BF),
            vmem((NCH, CH, DB), BF),
            vmem((DB, CH), F32),
            vmem((CH, DB), F32),
            dma((NP, 2)),
            dma((NCH, 2)),
            dma((NCH, 2, 2)),
            dma((NCH, 2, 2)),
            dma((NP, 4, 2, 2)),
            dma((NP, 4, 2, 2)),
            dma((NIT, 2, 2)),
            dma((NIT, 2, 2)),
            dma((NIT, 2, 2)),
            dma((NIT, 2, 2)),
            dma((NP, 4, 2, 2)),
            dma((NP, 4, 2, 2)),
            dma((2, 2)),
            dma((NCH, 2)),
            dma((NCH, 2)),
            dma((NCH, 2)),
        ],
        compiler_params=pltpu.CompilerParams(
            collective_id=0, has_side_effects=True, vmem_limit_bytes=62 * 2**20
        ),
        cost_estimate=pl.CostEstimate(flops=29 * 10**9, bytes_accessed=20 * 10**6, transcendentals=10**6),
        name="block",
    )(tokens, cotangent, up_weight, down_weight)
    return mlp, ig, ug.astype(F32), dg.astype(F32)


def solution(mesh):
    fine = Mesh(mesh.devices.reshape(4, 2, 4, 2, 2), AXES)
    rows = P(("dp", "x", "yl"), ("z", "yh"))
    return jax.shard_map(
        on_device,
        mesh=fine,
        in_specs=(rows, P(("z", "yh"), ("x", "yl")), P(("x", "yl"), ("z", "yh")), rows),
        out_specs=(rows, rows, P(("z", "yh"), ("x", "yl", "dp")), P(("x", "yl", "dp"), ("z", "yh"))),
        check_vma=False,
    )
```

```python
import functools

import jax
import jax.numpy as jnp
from jax import lax
from jax.experimental import pallas as pl
from jax.experimental.pallas import tpu as pltpu
from jax.sharding import Mesh, PartitionSpec as P

ROOT_HALF = 0.7071067811865476
DENSITY = 0.3989422804014327
AXES = ("z", "yh", "x", "yl", "dp")
BF, F32 = jnp.bfloat16, jnp.float32

NP = 4
AS = 2
TB = 32
TP = 8 * TB
DB = 768
HB = 1536
CH = 256
NCH = HB // CH
NIT = NP * NCH
ZB = TP // 4
TH = TB // 2
OPS = (
    "start", "merge", "gelu", "spread", "use", "w_far0", "w_far1", "w_sib0", "w_sib1", "w_wait",
    "ag0", "ag1", "ag2", "ag3", "ag_wait", "rs0", "rs1", "rs2", "rs3", "rs4", "dw", "fin", "nop",
)
STEPS = (
    320, 321, 323, 195, 352, 322, 353, 355, 163, 326, 384, 327, 385, 354, 192, 259,
    227, 160, 416, 417, 256, 358, 291, 387, 359, 196, 224, 448, 3, 386, 164, 288,
    0, 35, 260, 32, 419, 193, 325, 67, 324, 418, 228, 161, 64, 391, 390, 99,
    292, 4, 449, 6, 96, 10, 36, 9, 165, 38, 128, 42, 357, 356, 68, 257,
    225, 423, 41, 70, 197, 422, 74, 289, 7, 1, 229, 162, 73, 131, 100, 451,
    389, 39, 33, 261, 194, 388, 18, 102, 293, 5, 11, 71, 226, 23, 65, 22,
    258, 103, 37, 420, 421, 132, 290, 43, 8, 106, 97, 21, 134, 69, 75, 135,
    2, 450, 14, 40, 129, 13, 107, 138, 105, 72, 20, 12, 34, 139, 50, 104,
    16, 137, 101, 17, 66, 136, 482, 44, 483, 82, 19, 98, 133, 76, 514, 15,
    51, 130, 45, 108, 480, 481, 114, 47, 83, 515, 546, 55, 77, 140, 146, 640,
    52, 46, 513, 115, 578, 53, 109, 54, 547, 672, 512, 84, 147, 78, 141, 641,
    87, 579, 85, 116, 545, 110, 86, 544, 673, 48, 610, 119, 148, 142, 117, 79,
    642, 611, 118, 577, 576, 149, 151, 150, 111, 487, 674, 486, 49, 143, 643, 80,
    519, 518, 81, 609, 112, 675, 608, 113, 144, 644, 145, 484, 551, 485, 550, 676,
    516, 517, 645, 582, 583, 548, 549, 677, 614, 580, 581, 612, 615, 613,
)


def nt(a, b):
    return lax.dot_general(a, b, (((1,), (1,)), ((), ())), preferred_element_type=F32)


def tn(a, b):
    return lax.dot_general(a, b, (((0,), (0,)), ((), ())), preferred_element_type=F32)


def nn(a, b):
    return jnp.dot(a, b, preferred_element_type=F32)


def kernel(
    tok, cot, w1, w2, mlp, ig, ug, dg,
    tg, w1c, w2c, ph, r1, r2, ab, acc, py, e1, e2, f1, f2, st1, st2, rt1, rt2, ow1, ow2,
    own_sem, wl_sem, ws_sem, wr_sem, as_sem, ar_sem,
    zs_sem, zr_sem, gs_sem, gr_sem, ps_sem, pr_sem, ds_sem, dr_sem, os_sem, or_sem,
):
    z, yh, x, yl, k = (lax.axis_index(a) for a in AXES)
    y = yh * 2 + yl

    def up(v, n):
        return lax.rem(v + n, 4)

    z1, z2, z3 = up(z, 1), up(z, 2), up(z, 3)
    x1, x2, x3 = up(x, 1), up(x, 2), up(x, 3)
    y1, y3 = up(y, 1), up(y, 3)
    yh1, yl1, yh3, yl3 = y1 // 2, lax.rem(y1, 2), y3 // 2, lax.rem(y3, 2)
    yo, ko = 1 - yh, 1 - k
    z_dev = ((z1, yh, x, yl, k), (z3, yh, x, yl, k))
    x_dev = ((z, yh, x1, yl, k), (z, yh, x3, yl, k))
    y_dev = ((z, yh1, x, yl1, k), (z, yh3, x, yl3, k))
    far = (z, yo, x, yl, k)
    sib = (z, yh, x, yl, ko)
    diag = (z, yo, x, yl, ko)

    def send(src, dst, s_sem, r_sem, device):
        return pltpu.make_async_remote_copy(
            src_ref=src, dst_ref=dst, send_sem=s_sem, recv_sem=r_sem,
            device_id=device, device_id_type=pl.DeviceIdType.MESH,
        )

    def own(p, a):
        rows = pl.ds(pl.multiple_of(p * TB, TB), TB)
        return pltpu.make_async_copy((tok, cot)[a].at[rows], tg.at[a, yh, p, x, yl], own_sem.at[p, a])

    def hidden_at(half, c):
        return pl.multiple_of(half * HB + c * CH, CH)

    def w_own(c):
        return (
            pltpu.make_async_copy(w1.at[:, pl.ds(hidden_at(yh, c), CH)], w1c.at[c, yh], wl_sem.at[c, 0]),
            pltpu.make_async_copy(w2.at[pl.ds(hidden_at(yh, c), CH)], w2c.at[c, yh], wl_sem.at[c, 1]),
        )

    r_half = pl.ds(pl.multiple_of(k * (DB // 2), DB // 2), DB // 2)
    h_half = pl.ds(pl.multiple_of(k * (CH // 2), CH // 2), CH // 2)

    def w_far(c):
        rows = pl.ds(pl.multiple_of(yo * HB + c * CH + k * (CH // 2), CH // 2), CH // 2)
        return (
            send(w1.at[r_half, pl.ds(hidden_at(yo, c), CH)], w1c.at[c, yh, r_half],
                 ws_sem.at[c, 0, 0], wr_sem.at[c, 0, 0], far),
            send(w2.at[rows], w2c.at[c, yh, h_half], ws_sem.at[c, 0, 1], wr_sem.at[c, 0, 1], far),
        )

    def w_sib(c):
        return tuple(
            send(ref.at[c, yo, part], ref.at[c, yo, part], ws_sem.at[c, 1, a], wr_sem.at[c, 1, a], sib)
            for a, (ref, part) in enumerate(((w1c, r_half), (w2c, h_half)))
        )

    def ag(s, p, a):
        over = (y_dev, x_dev)[s // 2]
        if s == 0:
            parts = [tg.at[a, yh, p, x, yl]] * 2
        elif s == 1:
            parts = [tg.at[a, yh3, p, x, yl3, pl.ds(0, TH)], tg.at[a, yh1, p, x, yl1, pl.ds(TH, TH)]]
        elif s == 2:
            parts = [tg.at[a, :, p, x]] * 2
        else:
            parts = [tg.at[a, 0, p, x3], tg.at[a, 1, p, x1]]
        return [
            send(parts[d], parts[d], as_sem.at[p, s, a, d], ar_sem.at[p, s, a, d], over[d]) for d in range(2)
        ]

    def ag_step(s, arg):
        p, a = arg // 2, lax.rem(arg, 2)
        if s == 0:
            for b in range(2):
                @pl.when(a == b)
                def _():
                    own(p, b).wait()
        else:
            for copy in ag(s - 1, p, a):
                copy.wait_recv()
        for copy in ag(s, p, a):
            copy.start()

    def ag_wait(p):
        for a in range(2):
            for copy in ag(3, p, a):
                copy.wait_recv()

    def rs1(j):
        return [
            send(ph.at[j, :, z2, pl.ds(d * (ZB // 2), ZB // 2)], r1.at[j, d],
                 zs_sem.at[j, 0, d], zr_sem.at[j, 0, d], z_dev[d])
            for d in range(2)
        ]

    def rs2(j):
        return [
            send(ph.at[j, :, (z1, z3)[d]], r2.at[j, d], zs_sem.at[j, 1, d], zr_sem.at[j, 1, d], z_dev[d])
            for d in range(2)
        ]

    def ag1(j):
        p, c = j // NCH, lax.rem(j, NCH)
        part = ab.at[c, :, p, z]
        return [send(part, part, gs_sem.at[j, 0, d], gr_sem.at[j, 0, d], z_dev[d]) for d in range(2)]

    def ag2(j):
        p, c = j // NCH, lax.rem(j, NCH)
        parts = (
            ab.at[c, :, p, z3, pl.ds(0, ZB // 2)],
            ab.at[c, :, p, z1, pl.ds(ZB // 2, ZB // 2)],
        )
        return [
            send(parts[d], parts[d], gs_sem.at[j, 1, d], gr_sem.at[j, 1, d], z_dev[d]) for d in range(2)
        ]

    def start_item(j):
        p, c = j // NCH, lax.rem(j, NCH)
        h = nn(tg[0, 0, p].reshape(TP, DB), w1c[c, 0])
        h = h + nn(tg[0, 1, p].reshape(TP, DB), w1c[c, 1])
        ph[j, 0] = h.astype(BF).reshape(4, ZB, CH)
        s = nt(tg[1, 0, p].reshape(TP, DB), w2c[c, 0])
        s = s + nt(tg[1, 1, p].reshape(TP, DB), w2c[c, 1])
        ph[j, 1] = s.astype(BF).reshape(4, ZB, CH)
        for copy in rs1(j):
            copy.start()

    def merge_item(j):
        for d, (copy, go) in enumerate(zip(rs1(j), rs2(j))):
            copy.wait_recv()
            rows = pl.ds(d * (ZB // 2), ZB // 2)
            to = (z1, z3)[d]
            ph[j, :, to, rows] = (
                ph[j, :, to, rows].astype(F32) + r1[j, d].astype(F32)
            ).astype(BF)
            go.start()

    def gelu_item(j):
        p, c = j // NCH, lax.rem(j, NCH)
        for copy in rs2(j):
            copy.wait_recv()
        pre = ph[j, 0, z].astype(F32) + r2[j, 0, 0].astype(F32) + r2[j, 1, 0].astype(F32)
        back = ph[j, 1, z].astype(F32) + r2[j, 0, 1].astype(F32) + r2[j, 1, 1].astype(F32)
        cdf = 0.5 * (1.0 + lax.erf(pre * ROOT_HALF))
        ab[c, 0, p, z] = (pre * cdf).astype(BF)
        ab[c, 1, p, z] = (back * (cdf + pre * DENSITY * jnp.exp(-0.5 * pre * pre))).astype(BF)
        for copy in ag1(j):
            copy.start()

    def spread_item(j):
        for copy, go in zip(ag1(j), ag2(j)):
            copy.wait_recv()
            go.start()

    def to_sib(c):
        slot = lax.rem(c, 2)
        return (
            send(st1.at[slot], rt1.at[c], ds_sem.at[slot, 0], dr_sem.at[c, 0], sib),
            send(st2.at[slot], rt2.at[c], ds_sem.at[slot, 1], dr_sem.at[c, 1], sib),
        )

    def out_parts(c):
        hid = pl.ds(pl.multiple_of(c * CH, CH), CH)
        return ((rt1.at[c], ug.at[:, hid]), (rt2.at[c], dg.at[hid]))

    def out_local(c):
        return [pltpu.make_async_copy(s, d, os_sem.at[c, a]) for a, (s, d) in enumerate(out_parts(c))]

    def out_far(c):
        return [send(s, d, os_sem.at[c, a], or_sem.at[c, a], diag) for a, (s, d) in enumerate(out_parts(c))]

    def use_item(j):
        p, c = j // NCH, lax.rem(j, NCH)
        for copy in ag2(j):
            copy.wait_recv()
        act = ab[c, 0, p].reshape(TP, CH)
        hid = ab[c, 1, p].reshape(TP, CH)
        slot = lax.rem(p, AS)

        @pl.when(c == 0)
        def _():
            for half in range(2):
                acc[slot, 0, half] = nn(act, w2c[c, half])
                acc[slot, 1, half] = nt(hid, w1c[c, half])

        @pl.when(c > 0)
        def _():
            for half in range(2):
                acc[slot, 0, half] += nn(act, w2c[c, half])
                acc[slot, 1, half] += nt(hid, w1c[c, half])

    def grad_item(c):
        slot = lax.rem(c, 2)

        @pl.when(c >= 2)
        def _():
            for copy in to_sib(c - 2):
                copy.wait_send()

        acts = ab[c, 0].reshape(NP * TP, CH)
        hids = ab[c, 1].reshape(NP * TP, CH)
        st1[slot] = tn(tg[0, ko].reshape(NP * TP, DB), hids).astype(BF)
        st2[slot] = tn(acts, tg[1, ko].reshape(NP * TP, DB)).astype(BF)
        for copy in to_sib(c):
            copy.start()
        ow1[...] = tn(tg[0, k].reshape(NP * TP, DB), hids)
        ow2[...] = tn(acts, tg[1, k].reshape(NP * TP, DB))

    def finish_grad(c):
        for copy in to_sib(c):
            copy.wait_recv()
        rt1[c] = (rt1[c].astype(F32) + ow1[...]).astype(BF)
        rt2[c] = (rt2[c].astype(F32) + ow2[...]).astype(BF)

        @pl.when(k == yh)
        def _():
            for copy in out_local(c):
                copy.start()

        @pl.when(k != yh)
        def _():
            for copy in out_far(c):
                copy.start()

    def rs(s, p, a):
        over = (x_dev, y_dev)[s // 2]
        slot = lax.rem(p, AS)
        if s == 0:
            srcs = [py.at[slot, a, d, x2] for d in range(2)]
        elif s == 1:
            srcs = [py.at[slot, a, :, x1], py.at[slot, a, :, x3]]
        elif s == 2:
            srcs = [py.at[slot, a, yo, x, yl, pl.ds(d * TH, TH)] for d in range(2)]
        else:
            srcs = [py.at[slot, a, yh1, x, yl1], py.at[slot, a, yh3, x, yl3]]
        return [
            send(srcs[d], (e1, e2, f1, f2)[s].at[p, a, d], ps_sem.at[p, s, a, d], pr_sem.at[p, s, a, d], over[d])
            for d in range(2)
        ]

    def bump(ref, index, *more):
        total = ref[index].astype(F32)
        for term in more:
            total = total + term.astype(F32)
        ref[index] = total.astype(BF)

    def rs_step(s, arg):
        p, a = arg // 2, lax.rem(arg, 2)
        slot = lax.rem(p, AS)
        if s == 0:
            for half in range(2):
                py[slot, a, half] = acc[slot, a, half].astype(BF).reshape(4, 2, TB, DB)
        else:
            for copy in rs(s - 1, p, a):
                copy.wait_recv()
        if s == 1:
            bump(py, (slot, a, 0, x1), e1[p, a, 0])
            bump(py, (slot, a, 1, x3), e1[p, a, 1])
        elif s == 2:
            for half in range(2):
                bump(py, (slot, a, half, x), e2[p, a, 0, half], e2[p, a, 1, half])
        elif s == 3:
            bump(py, (slot, a, yh1, x, yl1, pl.ds(0, TH)), f1[p, a, 0])
            bump(py, (slot, a, yh3, x, yl3, pl.ds(TH, TH)), f1[p, a, 1])
        elif s == 4:
            rows = pl.ds(pl.multiple_of(p * TB, TB), TB)
            total = (
                py[slot, a, yh, x, yl].astype(F32) + f2[p, a, 0].astype(F32) + f2[p, a, 1].astype(F32)
            ).astype(BF)
            for b, out in enumerate((mlp, ig)):
                @pl.when(a == b)
                def _():
                    out[rows] = total
            for at in range(4):
                for copy in rs(at, p, a):
                    copy.wait_send()
        if s < 4:
            for copy in rs(s, p, a):
                copy.start()

    barrier = pltpu.get_barrier_semaphore()
    peers = (*z_dev, *x_dev, *y_dev, far, sib, diag)
    for p in range(NP):
        for a in range(2):
            own(p, a).start()
    for c in range(NCH):
        for copy in w_own(c):
            copy.start()
    for device in peers:
        pl.semaphore_signal(barrier, inc=1, device_id=device, device_id_type=pl.DeviceIdType.MESH)
    pl.semaphore_wait(barrier, len(peers))

    def w_far_step(a, c):
        w_far(c)[a].start()

    def w_sib_step(a, c):
        w_far(c)[a].wait_recv()
        w_sib(c)[a].start()

    def w_wait(c):
        for copy in w_own(c):
            copy.wait()
        for copy in w_sib(c):
            copy.wait_recv()

    runs = [start_item, merge_item, gelu_item, spread_item, use_item]
    runs += [functools.partial(w_far_step, a) for a in range(2)]
    runs += [functools.partial(w_sib_step, a) for a in range(2)]
    runs += [w_wait]
    runs += [functools.partial(ag_step, s) for s in range(4)]
    runs += [ag_wait]
    runs += [functools.partial(rs_step, s) for s in range(5)]
    runs += [grad_item, finish_grad]
    nop = OPS.index("nop")

    def dispatch(lo, hi, what, arg):
        if hi - lo == 1:
            if lo < nop:
                runs[lo](arg)
            return
        mid = (lo + hi) // 2

        @pl.when(what < mid)
        def _():
            dispatch(lo, mid, what, arg)

        @pl.when(what >= mid)
        def _():
            dispatch(mid, hi, what, arg)

    steps = list(STEPS) + [nop * 32] * (-len(STEPS) % 3)
    words = [steps[n] + steps[n + 1] * 1024 + steps[n + 2] * 1024 * 1024 for n in range(0, len(steps), 3)]

    def word(n, carry):
        value = jnp.int32(words[0])
        for at in range(1, len(words)):
            value = jnp.where(n == at, jnp.int32(words[at]), value)

        def step(_, left):
            now = lax.rem(left, 1024)
            dispatch(0, nop + 1, now // 32, lax.rem(now, 32))
            return left // 1024

        lax.fori_loop(0, 3, step, value)
        return carry

    lax.fori_loop(0, len(words), word, 0)

    def drain(j, carry):
        for copy in rs1(j) + rs2(j) + ag1(j) + ag2(j):
            copy.wait_send()

        @pl.when(j < NP * 2)
        def _():
            for s in range(4):
                for copy in ag(s, j // 2, lax.rem(j, 2)):
                    copy.wait_send()

        @pl.when(j < NCH)
        def _():
            for copy in w_far(j) + w_sib(j):
                copy.wait_send()

            @pl.when(j >= NCH - 2)
            def _():
                for copy in to_sib(j):
                    copy.wait_send()

            @pl.when(k == yh)
            def _():
                for copy in out_local(j):
                    copy.wait()

            @pl.when(k != yh)
            def _():
                for copy in out_far(j):
                    copy.wait()

        return carry

    lax.fori_loop(0, NIT, drain, 0)


def on_device(tokens, up_weight, down_weight, cotangent):
    vmem, dma = pltpu.VMEM, pltpu.SemaphoreType.DMA
    anywhere = pl.BlockSpec(memory_space=pl.ANY)
    inside = pl.BlockSpec(memory_space=pltpu.VMEM)

    mlp, ig, ug, dg = pl.pallas_call(
        kernel,
        out_shape=(
            jax.ShapeDtypeStruct((NP * TB, DB), BF),
            jax.ShapeDtypeStruct((NP * TB, DB), BF),
            jax.ShapeDtypeStruct((DB, HB), BF),
            jax.ShapeDtypeStruct((HB, DB), BF),
        ),
        in_specs=[anywhere] * 4,
        out_specs=(inside, inside, anywhere, anywhere),
        scratch_shapes=[
            vmem((2, 2, NP, 4, 2, TB, DB), BF),
            vmem((NCH, 2, DB, CH), BF),
            vmem((NCH, 2, CH, DB), BF),
            vmem((NIT, 2, 4, ZB, CH), BF),
            vmem((NIT, 2, 2, ZB // 2, CH), BF),
            vmem((NIT, 2, 2, ZB, CH), BF),
            vmem((NCH, 2, NP, 4, ZB, CH), BF),
            vmem((AS, 2, 2, TP, DB), F32),
            vmem((AS, 2, 2, 4, 2, TB, DB), BF),
            vmem((NP, 2, 2, 2, TB, DB), BF),
            vmem((NP, 2, 2, 2, 2, TB, DB), BF),
            vmem((NP, 2, 2, TH, DB), BF),
            vmem((NP, 2, 2, TB, DB), BF),
            vmem((2, DB, CH), BF),
            vmem((2, CH, DB), BF),
            vmem((NCH, DB, CH), BF),
            vmem((NCH, CH, DB), BF),
            vmem((DB, CH), F32),
            vmem((CH, DB), F32),
            dma((NP, 2)),
            dma((NCH, 2)),
            dma((NCH, 2, 2)),
            dma((NCH, 2, 2)),
            dma((NP, 4, 2, 2)),
            dma((NP, 4, 2, 2)),
            dma((NIT, 2, 2)),
            dma((NIT, 2, 2)),
            dma((NIT, 2, 2)),
            dma((NIT, 2, 2)),
            dma((NP, 4, 2, 2)),
            dma((NP, 4, 2, 2)),
            dma((2, 2)),
            dma((NCH, 2)),
            dma((NCH, 2)),
            dma((NCH, 2)),
        ],
        compiler_params=pltpu.CompilerParams(
            collective_id=0, has_side_effects=True, vmem_limit_bytes=62 * 2**20
        ),
        cost_estimate=pl.CostEstimate(flops=29 * 10**9, bytes_accessed=20 * 10**6, transcendentals=10**6),
        name="block",
    )(tokens, cotangent, up_weight, down_weight)
    return mlp, ig, ug.astype(F32), dg.astype(F32)


def solution(mesh):
    fine = Mesh(mesh.devices.reshape(4, 2, 4, 2, 2), AXES)
    rows = P(("dp", "x", "yl"), ("z", "yh"))
    return jax.shard_map(
        on_device,
        mesh=fine,
        in_specs=(rows, P(("z", "yh"), ("x", "yl")), P(("x", "yl"), ("z", "yh")), rows),
        out_specs=(rows, rows, P(("z", "yh"), ("x", "yl", "dp")), P(("x", "yl", "dp"), ("z", "yh"))),
        check_vma=False,
    )
```

```python
import functools

import jax
import jax.numpy as jnp
from jax import lax
from jax.experimental import pallas as pl
from jax.experimental.pallas import tpu as pltpu
from jax.sharding import Mesh, PartitionSpec as P

ROOT_HALF = 0.7071067811865476
DENSITY = 0.3989422804014327
AXES = ("z", "yh", "x", "yl", "dp")
BF, F32 = jnp.bfloat16, jnp.float32

NP = 4
AS = 2
TB = 32
TP = 8 * TB
DB = 768
HB = 1536
CH = 256
NCH = HB // CH
NIT = NP * NCH
ZB = TP // 4
TH = TB // 2
WB = 4
OPS = (
    "start", "merge", "gelu", "spread", "use", "w_far0", "w_far1", "w_sib0", "w_sib1", "w_wait",
    "ag0", "ag1", "ag2", "ag3", "ag_wait", "rs0", "rs1", "rs2", "rs3", "rs4", "dw", "fin", "nop",
)
STEPS = (
    320, 321, 323, 195, 352, 322, 353, 355, 163, 326, 384, 327, 385, 354, 192, 259,
    227, 160, 416, 417, 256, 358, 291, 387, 359, 196, 224, 448, 3, 386, 164, 288,
    0, 35, 260, 32, 419, 193, 325, 67, 324, 418, 228, 161, 64, 391, 390, 99,
    292, 4, 449, 6, 96, 10, 36, 9, 165, 38, 128, 42, 357, 356, 68, 257,
    225, 423, 41, 70, 197, 422, 74, 289, 7, 1, 229, 162, 73, 131, 100, 451,
    389, 39, 33, 261, 194, 388, 18, 102, 293, 5, 11, 71, 226, 23, 65, 22,
    258, 103, 37, 420, 421, 132, 290, 43, 8, 106, 97, 21, 134, 69, 75, 135,
    2, 450, 14, 40, 129, 13, 107, 138, 105, 72, 20, 12, 34, 139, 50, 104,
    16, 137, 101, 17, 66, 136, 482, 44, 483, 82, 19, 98, 133, 76, 514, 15,
    51, 130, 45, 108, 480, 481, 114, 47, 83, 515, 546, 55, 77, 140, 146, 640,
    52, 46, 513, 115, 578, 53, 109, 54, 547, 672, 512, 84, 147, 78, 141, 641,
    87, 579, 85, 116, 545, 110, 86, 544, 673, 48, 610, 119, 148, 142, 117, 79,
    642, 611, 118, 577, 576, 149, 151, 150, 111, 487, 674, 486, 49, 143, 643, 80,
    519, 518, 81, 609, 112, 675, 608, 113, 144, 644, 145, 484, 551, 485, 550, 676,
    516, 517, 645, 582, 583, 548, 549, 677, 614, 580, 581, 612, 615, 613,
)


def nt(a, b):
    return lax.dot_general(a, b, (((1,), (1,)), ((), ())), preferred_element_type=F32)


def tn(a, b):
    return lax.dot_general(a, b, (((0,), (0,)), ((), ())), preferred_element_type=F32)


def nn(a, b):
    return jnp.dot(a, b, preferred_element_type=F32)


def kernel(
    tok, cot, w1, w2, mlp, ig, ug, dg,
    tg, w1c, w2c, ph, r1, r2, ab, acc, py, e1, e2, f1, f2, st1, st2, rt1, rt2, ow1, ow2,
    own_sem, wl_sem, ws_sem, wr_sem, as_sem, ar_sem,
    zs_sem, zr_sem, gs_sem, gr_sem, ps_sem, pr_sem, ds_sem, dr_sem, os_sem, or_sem,
):
    z, yh, x, yl, k = (lax.axis_index(a) for a in AXES)
    y = yh * 2 + yl

    def up(v, n):
        return lax.rem(v + n, 4)

    z1, z2, z3 = up(z, 1), up(z, 2), up(z, 3)
    x1, x2, x3 = up(x, 1), up(x, 2), up(x, 3)
    y1, y3 = up(y, 1), up(y, 3)
    yh1, yl1, yh3, yl3 = y1 // 2, lax.rem(y1, 2), y3 // 2, lax.rem(y3, 2)
    yo, ko = 1 - yh, 1 - k
    z_dev = ((z1, yh, x, yl, k), (z3, yh, x, yl, k))
    x_dev = ((z, yh, x1, yl, k), (z, yh, x3, yl, k))
    y_dev = ((z, yh1, x, yl1, k), (z, yh3, x, yl3, k))
    far = (z, yo, x, yl, k)
    sib = (z, yh, x, yl, ko)
    diag = (z, yo, x, yl, ko)

    def send(src, dst, s_sem, r_sem, device):
        return pltpu.make_async_remote_copy(
            src_ref=src, dst_ref=dst, send_sem=s_sem, recv_sem=r_sem,
            device_id=device, device_id_type=pl.DeviceIdType.MESH,
        )

    def own(p, a):
        rows = pl.ds(pl.multiple_of(p * TB, TB), TB)
        return pltpu.make_async_copy((tok, cot)[a].at[rows], tg.at[a, yh, p, x, yl], own_sem.at[p, a])

    def hidden_at(half, c):
        return pl.multiple_of(half * HB + c * CH, CH)

    def w_own(c):
        return (
            pltpu.make_async_copy(w1.at[:, pl.ds(hidden_at(yh, c), CH)], w1c.at[c, yh], wl_sem.at[c, 0]),
            pltpu.make_async_copy(w2.at[pl.ds(hidden_at(yh, c), CH)], w2c.at[c, yh], wl_sem.at[c, 1]),
        )

    r_half = pl.ds(pl.multiple_of(k * (DB // 2), DB // 2), DB // 2)
    h_half = pl.ds(pl.multiple_of(k * (CH // 2), CH // 2), CH // 2)

    def w_far(c):
        rows = pl.ds(pl.multiple_of(yo * HB + c * CH + k * (CH // 2), CH // 2), CH // 2)
        return (
            send(w1.at[r_half, pl.ds(hidden_at(yo, c), CH)], w1c.at[c, yh, r_half],
                 ws_sem.at[c, 0, 0], wr_sem.at[c, 0, 0], far),
            send(w2.at[rows], w2c.at[c, yh, h_half], ws_sem.at[c, 0, 1], wr_sem.at[c, 0, 1], far),
        )

    def w_sib(c):
        return tuple(
            send(ref.at[c, yo, part], ref.at[c, yo, part], ws_sem.at[c, 1, a], wr_sem.at[c, 1, a], sib)
            for a, (ref, part) in enumerate(((w1c, r_half), (w2c, h_half)))
        )

    def ag(s, p, a):
        over = (y_dev, x_dev)[s // 2]
        if s == 0:
            parts = [tg.at[a, yh, p, x, yl]] * 2
        elif s == 1:
            parts = [tg.at[a, yh3, p, x, yl3, pl.ds(0, TH)], tg.at[a, yh1, p, x, yl1, pl.ds(TH, TH)]]
        elif s == 2:
            parts = [tg.at[a, :, p, x]] * 2
        else:
            parts = [tg.at[a, 0, p, x3], tg.at[a, 1, p, x1]]
        return [
            send(parts[d], parts[d], as_sem.at[p, s, a, d], ar_sem.at[p, s, a, d], over[d]) for d in range(2)
        ]

    def ag_step(s, arg):
        p, a = arg // 2, lax.rem(arg, 2)
        if s == 0:
            for b in range(2):
                @pl.when(a == b)
                def _():
                    own(p, b).wait()
        else:
            for copy in ag(s - 1, p, a):
                copy.wait_recv()
        for copy in ag(s, p, a):
            copy.start()

    def ag_wait(p):
        for a in range(2):
            for copy in ag(3, p, a):
                copy.wait_recv()

    def rs1(j):
        return [
            send(ph.at[j, :, z2, pl.ds(d * (ZB // 2), ZB // 2)], r1.at[j, d],
                 zs_sem.at[j, 0, d], zr_sem.at[j, 0, d], z_dev[d])
            for d in range(2)
        ]

    def rs2(j):
        return [
            send(ph.at[j, :, (z1, z3)[d]], r2.at[j, d], zs_sem.at[j, 1, d], zr_sem.at[j, 1, d], z_dev[d])
            for d in range(2)
        ]

    def ag1(j):
        p, c = j // NCH, lax.rem(j, NCH)
        part = ab.at[c, :, p, z]
        return [send(part, part, gs_sem.at[j, 0, d], gr_sem.at[j, 0, d], z_dev[d]) for d in range(2)]

    def ag2(j):
        p, c = j // NCH, lax.rem(j, NCH)
        parts = (
            ab.at[c, :, p, z3, pl.ds(0, ZB // 2)],
            ab.at[c, :, p, z1, pl.ds(ZB // 2, ZB // 2)],
        )
        return [
            send(parts[d], parts[d], gs_sem.at[j, 1, d], gr_sem.at[j, 1, d], z_dev[d]) for d in range(2)
        ]

    def start_item(j):
        p, c = j // NCH, lax.rem(j, NCH)
        h = nn(tg[0, 0, p].reshape(TP, DB), w1c[c, 0])
        h = h + nn(tg[0, 1, p].reshape(TP, DB), w1c[c, 1])
        ph[j, 0] = h.astype(BF).reshape(4, ZB, CH)
        s = nt(tg[1, 0, p].reshape(TP, DB), w2c[c, 0])
        s = s + nt(tg[1, 1, p].reshape(TP, DB), w2c[c, 1])
        ph[j, 1] = s.astype(BF).reshape(4, ZB, CH)
        for copy in rs1(j):
            copy.start()

    def merge_item(j):
        for d, (copy, go) in enumerate(zip(rs1(j), rs2(j))):
            copy.wait_recv()
            rows = pl.ds(d * (ZB // 2), ZB // 2)
            to = (z1, z3)[d]
            ph[j, :, to, rows] = (
                ph[j, :, to, rows].astype(F32) + r1[j, d].astype(F32)
            ).astype(BF)
            go.start()

    def gelu_item(j):
        p, c = j // NCH, lax.rem(j, NCH)
        for copy in rs2(j):
            copy.wait_recv()
        pre = ph[j, 0, z].astype(F32) + r2[j, 0, 0].astype(F32) + r2[j, 1, 0].astype(F32)
        back = ph[j, 1, z].astype(F32) + r2[j, 0, 1].astype(F32) + r2[j, 1, 1].astype(F32)
        cdf = 0.5 * (1.0 + lax.erf(pre * ROOT_HALF))
        ab[c, 0, p, z] = (pre * cdf).astype(BF)
        ab[c, 1, p, z] = (back * (cdf + pre * DENSITY * jnp.exp(-0.5 * pre * pre))).astype(BF)
        for copy in ag1(j):
            copy.start()

    def spread_item(j):
        for copy, go in zip(ag1(j), ag2(j)):
            copy.wait_recv()
            go.start()

    def to_sib(c):
        slot = lax.rem(c, 2)
        return (
            send(st1.at[slot], rt1.at[c], ds_sem.at[slot, 0], dr_sem.at[c, 0], sib),
            send(st2.at[slot], rt2.at[c], ds_sem.at[slot, 1], dr_sem.at[c, 1], sib),
        )

    def out_parts(c):
        hid = pl.ds(pl.multiple_of(c * CH, CH), CH)
        return ((rt1.at[c], ug.at[:, hid]), (rt2.at[c], dg.at[hid]))

    def out_local(c):
        return [pltpu.make_async_copy(s, d, os_sem.at[c, a]) for a, (s, d) in enumerate(out_parts(c))]

    def out_far(c):
        return [send(s, d, os_sem.at[c, a], or_sem.at[c, a], diag) for a, (s, d) in enumerate(out_parts(c))]

    def use_item(j):
        p, c = j // NCH, lax.rem(j, NCH)
        for copy in ag2(j):
            copy.wait_recv()
        act = ab[c, 0, p].reshape(TP, CH)
        hid = ab[c, 1, p].reshape(TP, CH)
        slot = lax.rem(p, AS)

        @pl.when(c == 0)
        def _():
            for half in range(2):
                acc[slot, 0, half] = nn(act, w2c[c, half])
                acc[slot, 1, half] = nt(hid, w1c[c, half])

        @pl.when(c > 0)
        def _():
            for half in range(2):
                acc[slot, 0, half] += nn(act, w2c[c, half])
                acc[slot, 1, half] += nt(hid, w1c[c, half])

    def grad_item(c):
        slot = lax.rem(c, 2)

        @pl.when(c >= 2)
        def _():
            for copy in to_sib(c - 2):
                copy.wait_send()

        acts = ab[c, 0].reshape(NP * TP, CH)
        hids = ab[c, 1].reshape(NP * TP, CH)
        st1[slot] = tn(tg[0, ko].reshape(NP * TP, DB), hids).astype(BF)
        st2[slot] = tn(acts, tg[1, ko].reshape(NP * TP, DB)).astype(BF)
        for copy in to_sib(c):
            copy.start()
        ow1[...] = tn(tg[0, k].reshape(NP * TP, DB), hids)
        ow2[...] = tn(acts, tg[1, k].reshape(NP * TP, DB))

    def finish_grad(c):
        for copy in to_sib(c):
            copy.wait_recv()
        rt1[c] = (rt1[c].astype(F32) + ow1[...]).astype(BF)
        rt2[c] = (rt2[c].astype(F32) + ow2[...]).astype(BF)

        @pl.when(k == yh)
        def _():
            for copy in out_local(c):
                copy.start()

        @pl.when(k != yh)
        def _():
            for copy in out_far(c):
                copy.start()

    def rs(s, p, a):
        over = (x_dev, y_dev)[s // 2]
        slot = lax.rem(p, AS)
        if s == 0:
            srcs = [py.at[slot, a, d, x2] for d in range(2)]
        elif s == 1:
            srcs = [py.at[slot, a, :, x1], py.at[slot, a, :, x3]]
        elif s == 2:
            srcs = [py.at[slot, a, yo, x, yl, pl.ds(d * TH, TH)] for d in range(2)]
        else:
            srcs = [py.at[slot, a, yh1, x, yl1], py.at[slot, a, yh3, x, yl3]]
        return [
            send(srcs[d], (e1, e2, f1, f2)[s].at[p, a, d], ps_sem.at[p, s, a, d], pr_sem.at[p, s, a, d], over[d])
            for d in range(2)
        ]

    def bump(ref, index, *more):
        total = ref[index].astype(F32)
        for term in more:
            total = total + term.astype(F32)
        ref[index] = total.astype(BF)

    def rs_step(s, arg):
        p, a = arg // 2, lax.rem(arg, 2)
        slot = lax.rem(p, AS)
        if s == 0:
            for half in range(2):
                py[slot, a, half] = acc[slot, a, half].astype(BF).reshape(4, 2, TB, DB)
        else:
            for copy in rs(s - 1, p, a):
                copy.wait_recv()
        if s == 1:
            bump(py, (slot, a, 0, x1), e1[p, a, 0])
            bump(py, (slot, a, 1, x3), e1[p, a, 1])
        elif s == 2:
            for half in range(2):
                bump(py, (slot, a, half, x), e2[p, a, 0, half], e2[p, a, 1, half])
        elif s == 3:
            bump(py, (slot, a, yh1, x, yl1, pl.ds(0, TH)), f1[p, a, 0])
            bump(py, (slot, a, yh3, x, yl3, pl.ds(TH, TH)), f1[p, a, 1])
        elif s == 4:
            rows = pl.ds(pl.multiple_of(p * TB, TB), TB)
            total = (
                py[slot, a, yh, x, yl].astype(F32) + f2[p, a, 0].astype(F32) + f2[p, a, 1].astype(F32)
            ).astype(BF)
            for b, out in enumerate((mlp, ig)):
                @pl.when(a == b)
                def _():
                    out[rows] = total
            for at in range(4):
                for copy in rs(at, p, a):
                    copy.wait_send()
        if s < 4:
            for copy in rs(s, p, a):
                copy.start()

    barrier = pltpu.get_barrier_semaphore()
    peers = (*z_dev, *x_dev, *y_dev, far, sib, diag)
    for p in range(NP):
        for a in range(2):
            own(p, a).start()
    for c in range(NCH):
        for copy in w_own(c):
            copy.start()
    for device in peers:
        pl.semaphore_signal(barrier, inc=1, device_id=device, device_id_type=pl.DeviceIdType.MESH)
    pl.semaphore_wait(barrier, len(peers))

    def w_far_step(a, c):
        w_far(c)[a].start()

    def w_sib_step(a, c):
        w_far(c)[a].wait_recv()
        w_sib(c)[a].start()

    def w_wait(c):
        for copy in w_own(c):
            copy.wait()
        for copy in w_sib(c):
            copy.wait_recv()

    runs = [start_item, merge_item, gelu_item, spread_item, use_item]
    runs += [functools.partial(w_far_step, a) for a in range(2)]
    runs += [functools.partial(w_sib_step, a) for a in range(2)]
    runs += [w_wait]
    runs += [functools.partial(ag_step, s) for s in range(4)]
    runs += [ag_wait]
    runs += [functools.partial(rs_step, s) for s in range(5)]
    runs += [grad_item, finish_grad]
    nop = OPS.index("nop")

    def dispatch(lo, hi, what, arg):
        if hi - lo == 1:
            if lo < nop:
                runs[lo](arg)
            return
        mid = (lo + hi) // 2

        @pl.when(what < mid)
        def _():
            dispatch(lo, mid, what, arg)

        @pl.when(what >= mid)
        def _():
            dispatch(mid, hi, what, arg)

    steps = list(STEPS) + [nop * 32] * (-len(STEPS) % 3)
    words = [steps[n] + steps[n + 1] * 1024 + steps[n + 2] * 1024 * 1024 for n in range(0, len(steps), 3)]

    def word(n, carry):
        value = jnp.int32(words[0])
        for at in range(1, len(words)):
            value = jnp.where(n == at, jnp.int32(words[at]), value)

        def step(_, left):
            now = lax.rem(left, 1024)
            dispatch(0, nop + 1, now // 32, lax.rem(now, 32))
            return left // 1024

        lax.fori_loop(0, 3, step, value)
        return carry

    lax.fori_loop(0, len(words), word, 0)

    def drain(j, carry):
        for copy in rs1(j) + rs2(j) + ag1(j) + ag2(j):
            copy.wait_send()

        @pl.when(j < NP * 2)
        def _():
            for s in range(4):
                for copy in ag(s, j // 2, lax.rem(j, 2)):
                    copy.wait_send()

        @pl.when(j < NCH)
        def _():
            for copy in w_far(j) + w_sib(j):
                copy.wait_send()

            @pl.when(j >= NCH - 2)
            def _():
                for copy in to_sib(j):
                    copy.wait_send()

            @pl.when(k == yh)
            def _():
                for copy in out_local(j):
                    copy.wait()

            @pl.when(k != yh)
            def _():
                for copy in out_far(j):
                    copy.wait()

        return carry

    lax.fori_loop(0, NIT, drain, 0)


def widen(mlp, ig, ug, dg, mlp_out, ig_out, ug_out, dg_out):
    mlp_out[...] = mlp[...]
    ig_out[...] = ig[...]
    ug_out[...] = ug[...].astype(F32)
    dg_out[...] = dg[...].astype(F32)


def on_device(tokens, up_weight, down_weight, cotangent):
    vmem, dma = pltpu.VMEM, pltpu.SemaphoreType.DMA
    anywhere = pl.BlockSpec(memory_space=pl.ANY)
    inside = pl.BlockSpec(memory_space=pltpu.VMEM)

    mlp, ig, ug, dg = pl.pallas_call(
        kernel,
        out_shape=(
            jax.ShapeDtypeStruct((NP * TB, DB), BF),
            jax.ShapeDtypeStruct((NP * TB, DB), BF),
            jax.ShapeDtypeStruct((DB, HB), BF),
            jax.ShapeDtypeStruct((HB, DB), BF),
        ),
        in_specs=[anywhere] * 4,
        out_specs=(inside, inside, anywhere, anywhere),
        scratch_shapes=[
            vmem((2, 2, NP, 4, 2, TB, DB), BF),
            vmem((NCH, 2, DB, CH), BF),
            vmem((NCH, 2, CH, DB), BF),
            vmem((NIT, 2, 4, ZB, CH), BF),
            vmem((NIT, 2, 2, ZB // 2, CH), BF),
            vmem((NIT, 2, 2, ZB, CH), BF),
            vmem((NCH, 2, NP, 4, ZB, CH), BF),
            vmem((AS, 2, 2, TP, DB), F32),
            vmem((AS, 2, 2, 4, 2, TB, DB), BF),
            vmem((NP, 2, 2, 2, TB, DB), BF),
            vmem((NP, 2, 2, 2, 2, TB, DB), BF),
            vmem((NP, 2, 2, TH, DB), BF),
            vmem((NP, 2, 2, TB, DB), BF),
            vmem((2, DB, CH), BF),
            vmem((2, CH, DB), BF),
            vmem((NCH, DB, CH), BF),
            vmem((NCH, CH, DB), BF),
            vmem((DB, CH), F32),
            vmem((CH, DB), F32),
            dma((NP, 2)),
            dma((NCH, 2)),
            dma((NCH, 2, 2)),
            dma((NCH, 2, 2)),
            dma((NP, 4, 2, 2)),
            dma((NP, 4, 2, 2)),
            dma((NIT, 2, 2)),
            dma((NIT, 2, 2)),
            dma((NIT, 2, 2)),
            dma((NIT, 2, 2)),
            dma((NP, 4, 2, 2)),
            dma((NP, 4, 2, 2)),
            dma((2, 2)),
            dma((NCH, 2)),
            dma((NCH, 2)),
            dma((NCH, 2)),
        ],
        compiler_params=pltpu.CompilerParams(
            collective_id=0, has_side_effects=True, vmem_limit_bytes=62 * 2**20
        ),
        cost_estimate=pl.CostEstimate(flops=29 * 10**9, bytes_accessed=20 * 10**6, transcendentals=10**6),
        name="block",
    )(tokens, cotangent, up_weight, down_weight)
    return pl.pallas_call(
        widen,
        grid=(WB,),
        out_shape=(
            jax.ShapeDtypeStruct(mlp.shape, BF),
            jax.ShapeDtypeStruct(ig.shape, BF),
            jax.ShapeDtypeStruct(ug.shape, F32),
            jax.ShapeDtypeStruct(dg.shape, F32),
        ),
        in_specs=[pl.BlockSpec((a.shape[0] // WB, a.shape[1]), lambda n: (n, 0)) for a in (mlp, ig, ug, dg)],
        out_specs=tuple(
            pl.BlockSpec((a.shape[0] // WB, a.shape[1]), lambda n: (n, 0)) for a in (mlp, ig, ug, dg)
        ),
        name="widen",
    )(mlp, ig, ug, dg)


def solution(mesh):
    fine = Mesh(mesh.devices.reshape(4, 2, 4, 2, 2), AXES)
    rows = P(("dp", "x", "yl"), ("z", "yh"))
    return jax.shard_map(
        on_device,
        mesh=fine,
        in_specs=(rows, P(("z", "yh"), ("x", "yl")), P(("x", "yl"), ("z", "yh")), rows),
        out_specs=(rows, rows, P(("z", "yh"), ("x", "yl", "dp")), P(("x", "yl", "dp"), ("z", "yh"))),
        check_vma=False,
    )
```
